32 devices in a mesh: src: 8 (over z, core), tgt: 4 (over y, x).
Axes of the slice: x: 2, y: 2, z: 4, core: 2. Of those that a mesh axis runs over, the one named last changes fastest.
Arguments:
- src_emb: bfloat16 [8192, 768], P(('src', 'tgt')), may hold values from -0.05119037 to 0.05119037
- right_sentence_vectors: bfloat16 [4096, 768], P(('tgt', 'src')), may hold values from -0.05119037 to 0.05119037
- src_mass: float32 [8192], P('src'), may hold values from 0.25 to 4
- tgt_mass: float32 [4096], P('tgt'), may hold values from 0.5 to 8
Outputs:
- grad_src: float32 [8192, 768], P(('src', 'tgt'))
- grad_tgt: float32 [4096, 768], P(('tgt', 'src'))
The draws below stay inside these ranges and needn't reach their ends.
All inputs are finite; a program needn't handle non-finite values.
Results may differ from the reference program's by a relative error of at most 0.00045.
Values may be sent and summed in bfloat16 or wider, within the bound.
A program may use at most 64 MiB of HBM per device.

```python
import math
import jax
import jax.numpy as jnp
from jax import lax

D = 768
ITERS = 4
NS = 8192
NT = 4096


def shared_direction(key):
    amplitude = (0.7 / D) ** 0.5
    signs = jax.random.bernoulli(jax.random.fold_in(key, 7), 0.5, (D,))
    magnitude = amplitude * jnp.ones((D,), jnp.float32)
    return jnp.where(signs, magnitude, -magnitude).astype(jnp.float32)


def placed_rows(key, count, salt):
    direction = shared_direction(key)
    position = (jnp.arange(count, dtype=jnp.float32) + 0.5) / count * 2.0 - 1.0
    jitter = jax.random.uniform(jax.random.fold_in(key, salt), (count,), jnp.float32, -0.2, 0.2)
    level = 0.8 * position + jitter
    noise = jax.random.uniform(jax.random.fold_in(key, salt + 1), (count, D), jnp.float32, -0.02, 0.02)
    return level[:, None] * direction[None, :] + noise


def draw_src_emb(key, part):
    return placed_rows(key, NS, 11).astype(jnp.bfloat16)


def draw_right_sentence_vectors(key, part):
    return placed_rows(key, NT, 23).astype(jnp.bfloat16)


def level_of(rng, extent, split, smallest, largest):
    factor_of, own = 1.0, jax.random.fold_in(rng, 6)
    for axis_at, shards_of in split:
        steps = jnp.exp(jax.random.uniform(jax.random.fold_in(own, axis_at), (shards_of,), jnp.float32, smallest / len(split), largest / len(split)))
        factor_of = factor_of * jnp.repeat(steps, extent[axis_at] // shards_of).reshape([-1 if axis == axis_at else 1 for axis in range(len(extent))])
    return factor_of


def setup_inputs(seed: int = 0) -> dict:
    key_of = jax.random.split(jax.random.key(seed), 5)
    src_emb = draw_src_emb(jax.random.fold_in(key_of[4], 71), 0)
    right_sentence_vectors = draw_right_sentence_vectors(jax.random.fold_in(key_of[4], 71), 0)
    src_mass = jnp.clip(jnp.exp(math.log(4.0) - 2.7725887 * jax.random.uniform(key_of[2], (NS,), jnp.float32) ** level_of(key_of[2], (NS,), ((0, 8),), -0.2, 0.2)), 0.25, 4.0)
    tgt_mass = jnp.clip(jnp.exp(math.log(8.0) - 2.7725887 * jax.random.uniform(key_of[3], (NT,), jnp.float32) ** level_of(key_of[3], (NT,), ((0, 4),), -0.2, 0.2)), 0.5, 8.0)
    return dict(src_emb=src_emb, right_sentence_vectors=right_sentence_vectors, src_mass=src_mass, tgt_mass=tgt_mass)


regularizer_epsilon = 0.05
highest = lax.Precision.HIGHEST


def make_tile(tile_window, right_sentence_vectors):
    kernel_grid = jnp.dot(tile_window, right_sentence_vectors.T, preferred_element_type=jnp.float32) / regularizer_epsilon
    kernel = lax.optimization_barrier(jnp.exp(kernel_grid).astype(jnp.bfloat16))
    return kernel_grid, kernel


def reference(src_emb, right_sentence_vectors, src_mass, tgt_mass):
    all_rows = src_emb.shape[0]
    block_rows = math.gcd(all_rows, 2048)
    block_count = all_rows // block_rows
    blocks = src_emb.reshape(block_count, block_rows, src_emb.shape[1])
    zeros_tgt = jnp.zeros(right_sentence_vectors.shape[0], jnp.float32)

    def row_pass(vector):
        def per_block(tile_window):
            kernel_grid, kernel = make_tile(tile_window, right_sentence_vectors)
            return jnp.dot(kernel, vector, precision=highest, preferred_element_type=jnp.float32)
        return lax.map(per_block, blocks).reshape(all_rows)

    def col_pass(vector):
        pieces = vector.reshape(block_count, block_rows)

        def per_block(running, member):
            kernel_grid, kernel = make_tile(member[0], right_sentence_vectors)
            return running + jnp.dot(member[1], kernel, precision=highest, preferred_element_type=jnp.float32), None
        result, unused = lax.scan(per_block, zeros_tgt, (blocks, pieces))
        return result

    vector = jnp.ones(right_sentence_vectors.shape[0], jnp.float32)
    old_saved, row_saved, src_saved, col_saved, tgt_saved = [], [], [], [], []
    for iteration in range(ITERS):
        old_saved.append(vector)
        row_total = row_pass(vector)
        src_scale = src_mass / row_total
        col_total = col_pass(src_scale)
        vector = tgt_mass / col_total
        row_saved.append(row_total)
        src_saved.append(src_scale)
        col_saved.append(col_total)
        tgt_saved.append(vector)
    last_src = src_saved[-1]
    last_tgt = tgt_saved[-1]

    def first_block(running, member):
        kernel_grid, kernel = make_tile(member[0], right_sentence_vectors)
        weighted = kernel * kernel_grid
        row_part = jnp.dot(weighted, last_tgt, precision=highest, preferred_element_type=jnp.float32)
        col_part = jnp.dot(member[1], weighted, precision=highest, preferred_element_type=jnp.float32)
        return running + col_part, row_part

    tgt_adj, row_parts = lax.scan(first_block, zeros_tgt, (blocks, last_src.reshape(block_count, block_rows)))
    src_adj = row_parts.reshape(all_rows)
    row_bars = [None] * ITERS
    col_bars = [None] * ITERS
    for iteration in reversed(range(ITERS)):
        col_bar = -tgt_adj * tgt_saved[iteration] / col_saved[iteration]
        back = row_pass(col_bar)
        if iteration == ITERS - 1:
            back = back + src_adj
        row_bar = -back * src_saved[iteration] / row_saved[iteration]
        if iteration > 0:
            tgt_adj = col_pass(row_bar)
        row_bars[iteration] = row_bar
        col_bars[iteration] = col_bar
    left = jnp.stack(row_bars + src_saved, axis=1)
    right = jnp.stack(old_saved + col_bars, axis=1)

    def grad_block(running, member):
        tile_window, left_rows, scale_rows = member
        kernel_grid, kernel = make_tile(tile_window, right_sentence_vectors)
        lowrank = jnp.dot(left_rows, right.T, precision=highest, preferred_element_type=jnp.float32)
        cross_term_grid = (kernel * (scale_rows[:, None] * last_tgt[None, :] * (1.0 + kernel_grid) + lowrank)).astype(jnp.bfloat16)
        left_share_piece = jnp.dot(cross_term_grid, right_sentence_vectors, preferred_element_type=jnp.float32) / regularizer_epsilon
        right_share_piece = lax.dot_general(cross_term_grid, tile_window, (((0,), (0,)), ((), ())), preferred_element_type=jnp.float32) / regularizer_epsilon
        return running + right_share_piece, left_share_piece

    zeros_grad = jnp.zeros(right_sentence_vectors.shape, jnp.float32)
    members = (blocks, left.reshape(block_count, block_rows, left.shape[1]), last_src.reshape(block_count, block_rows))
    grad_tgt, src_parts = lax.scan(grad_block, zeros_grad, members)
    return src_parts.reshape(all_rows, src_emb.shape[1]), grad_tgt
```

```python
import functools
import jax
import jax.numpy as jnp
from jax import lax
from jax.experimental import pallas as pl
from jax.experimental.pallas import tpu as pltpu
from jax.sharding import PartitionSpec as P

ITERS = 4
SCALE = 20.0
F32 = jnp.float32
BF16 = jnp.bfloat16
NN = (((1,), (0,)), ((), ()))
NT = (((1,), (1,)), ((), ()))
TN = (((0,), (0,)), ((), ()))
MESH = pl.DeviceIdType.MESH


def dot(a, b, dims):
    return lax.dot_general(a, b, dims, preferred_element_type=F32)


def split3(x):
    hi = x.astype(BF16).astype(F32)
    rest = x - hi
    mid = rest.astype(BF16).astype(F32)
    low = (rest - mid).astype(BF16).astype(F32)
    return hi, mid, low


def three_rows(x):
    hi, mid, low = split3(x)
    shape = (16, x.shape[1])
    row = lax.broadcasted_iota(jnp.int32, shape, 0)
    full = [jnp.broadcast_to(p, shape) for p in (hi, mid, low)]
    zero = jnp.zeros(shape, F32)
    return jnp.where(
        row == 0, full[0], jnp.where(row == 1, full[1], jnp.where(row == 2, full[2], zero))
    ).astype(BF16)


def body(
    ns, nt, src_ref, tgt_ref, smass_ref, tmass_ref, out_s, out_t,
    sr, tr, aff, ker, w1, w2, mix, lpart, rpair, rpart, lgot, rcore, rgot,
    ru, vc, rsum, csum, rbuf, cbuf, cbuf4,
    gs_send, gs_recv, gt_send, gt_recv, gc_send, gc_recv,
    r_send, r_recv, c_send, c_recv, c4_send, c4_recv,
    l_send, l_recv, x_send, x_recv, z_send, z_recv,
):
    me_t = lax.axis_index("tgt")
    me_s = lax.axis_index("src")
    nz = ns // 2
    core = lax.rem(me_s, 2)
    me_z = lax.div(me_s, 2)
    other = me_z * 2 + (1 - core)
    bs, d = src_ref.shape
    bt = tgt_ref.shape[0]
    rows, cols = nt * bs, ns * bt

    def peer_t(k):
        return lax.rem(me_t + k, nt)

    def peer_s(k):
        return lax.rem(me_s + k, ns)

    def peer_z(k):
        return lax.rem(me_z + k, nz)

    barrier = pltpu.get_barrier_semaphore()
    for k in range(1, nt):
        pl.semaphore_signal(barrier, inc=1, device_id=(me_s, peer_t(k)), device_id_type=MESH)
    for k in range(1, ns):
        pl.semaphore_signal(barrier, inc=1, device_id=(peer_s(k), me_t), device_id_type=MESH)
    pl.semaphore_wait(barrier, nt + ns - 2)

    def send(src, dst, s_sem, r_sem, dev):
        return pltpu.make_async_remote_copy(
            src_ref=src, dst_ref=dst, send_sem=s_sem, recv_sem=r_sem,
            device_id=dev, device_id_type=MESH,
        )

    gz = [
        send(tgt_ref, tr.at[me_s], gt_send.at[k], gt_recv.at[k], (peer_z(k) * 2 + core, me_t))
        for k in range(1, nz)
    ]
    gt = [
        send(src_ref, sr.at[me_t], gs_send.at[k], gs_recv.at[k], (me_s, peer_t(k)))
        for k in range(1, nt)
    ]
    for c in gz + gt:
        c.start()
    fwd = [send(tgt_ref, tr.at[me_s], gc_send.at[0], gc_recv.at[0], (other, me_t))]
    fwd[0].start()
    sr[me_t] = src_ref[...]
    tr[me_s] = tgt_ref[...]
    for k in range(1, nz):
        gz[k - 1].wait_recv()
        blk = lax.rem(me_z + nz - k, nz) * 2 + core
        c = send(tr.at[blk], tr.at[blk], gc_send.at[k], gc_recv.at[k], (other, me_t))
        c.start()
        fwd.append(c)
    for c in gt + fwd:
        c.wait()
    for c in gz:
        c.wait_send()

    def build(i, carry):
        a = dot(sr[i], tr[...].reshape(cols, d), NT) * SCALE
        kb = jnp.exp(a).astype(BF16)
        ker[i] = kb
        aff[i] = a
        w = kb.astype(F32) * a
        h = w.astype(BF16)
        w1[i] = h
        w2[i] = (w - h.astype(F32)).astype(BF16)
        return carry

    lax.fori_loop(0, nt, build, 0)

    def row_pass(m, x):
        return jnp.sum(dot(three_rows(x), m[...].reshape(rows, cols), NT), axis=0, keepdims=True)

    def col_pass(m, x):
        return jnp.sum(dot(three_rows(x), m[...].reshape(rows, cols), NN), axis=0, keepdims=True)

    def row_total(step, part):
        rbuf[step, me_t] = part
        cs = [
            send(rbuf.at[step, me_t], rbuf.at[step, me_t], r_send.at[step, k], r_recv.at[step, k],
                 (me_s, peer_t(k)))
            for k in range(1, nt)
        ]
        for c in cs:
            c.start()
        for c in cs:
            c.wait()
        total = rbuf[step, 0]
        for i in range(1, nt):
            total = total + rbuf[step, i]
        return total

    def col_start(buf, send_sem, recv_sem):
        cs = [
            send(buf.at[me_s], buf.at[me_s], send_sem.at[k], recv_sem.at[k], (peer_s(k), me_t))
            for k in range(1, ns)
        ]
        for c in cs:
            c.start()
        for c in cs:
            c.wait()
        total = buf[0]
        for i in range(1, ns):
            total = total + buf[i]
        return total

    def col_total(step, part):
        cbuf[step, me_s] = part
        return col_start(cbuf.at[step], c_send.at[step], c_recv.at[step])

    vc[pl.ds(0, 1), :] = jnp.ones((1, cols), F32)

    def scale_src(k):
        r = row_total(k, row_pass(ker, vc[pl.ds(k, 1), :]))
        u = smass_ref[...] / r
        rsum[pl.ds(k, 1), :] = r
        ru[pl.ds(ITERS + k, 1), :] = u
        return u

    def forward(k, carry):
        u = scale_src(k)
        c = col_total(k, col_pass(ker, u))
        csum[pl.ds(k, 1), :] = c
        vc[pl.ds(k + 1, 1), :] = tmass_ref[...] / c
        return carry

    lax.fori_loop(0, ITERS - 1, forward, 0)
    last = ITERS - 1
    u4 = scale_src(last)
    cbuf4[me_s, :, pl.ds(0, cols)] = col_pass(ker, u4)
    cbuf4[me_s, :, pl.ds(cols, cols)] = col_pass(w1, u4) + col_pass(w2, u4)
    both = col_start(cbuf4, c4_send, c4_recv)
    c4, tgt_adj = both[:, :cols], both[:, cols:]
    v4 = tmass_ref[...] / c4
    cbar = -tgt_adj * v4 / c4
    vc[pl.ds(ITERS + last, 1), :] = cbar
    part = row_pass(ker, cbar) + (row_pass(w1, v4) + row_pass(w2, v4))

    def rbar_of(k, part):
        back = row_total(ITERS + k, part)
        rbar = -back * ru[pl.ds(ITERS + k, 1), :] / rsum[pl.ds(k, 1), :]
        ru[pl.ds(k, 1), :] = rbar
        return rbar

    rbar = rbar_of(last, part)

    def backward(j, rbar):
        k = last - 1 - j
        adj = col_total(last + j, col_pass(ker, rbar))
        cbar = -adj * vc[pl.ds(k + 1, 1), :] / csum[pl.ds(k, 1), :]
        vc[pl.ds(ITERS + k, 1), :] = cbar
        return rbar_of(k, row_pass(ker, cbar))

    lax.fori_loop(0, ITERS - 1, backward, rbar)

    lh, lm, ll = split3(ru[...])
    rh, rm, rl = split3(vc[...])
    zero = jnp.zeros((8, cols), F32)
    lstack = jnp.concatenate(
        [lh, lh, lm, lm, lh, ll, jnp.broadcast_to(u4, (8, rows)), jnp.zeros((8, rows), F32)], axis=0
    )
    lcol = lstack.T
    rstack = jnp.concatenate([rh, rm, rh, rm, rl, rh, zero, zero], axis=0).astype(BF16)
    for i in range(nt):
        blk = lcol[i * bs:(i + 1) * bs]
        lk = blk.astype(BF16)
        low = dot(lk, rstack, NN)
        ucol = blk[:, 48:49]
        m = ker[i].astype(F32) * (ucol * v4 * (1.0 + aff[i]) + low)
        mix[i] = m.astype(BF16)

    lcopies = []
    for k in list(range(1, nt)):
        i = peer_t(k)
        lpart[k] = dot(mix[i], tr[...].reshape(cols, d), NN) * SCALE
        c = send(lpart.at[k], lgot.at[k], l_send.at[k], l_recv.at[k], (me_s, i))
        c.start()
        lcopies.append(c)

    xcopies = []
    for k in range(nz):
        z = peer_z(k + 1)
        m = mix[:, :, pl.ds(pl.multiple_of(z * (2 * bt), 2 * bt), 2 * bt)].reshape(rows, 2 * bt)
        pair = dot(m, sr[...].reshape(rows, d), TN) * SCALE
        rpair[k] = pair.reshape(2, bt, d)
        c = send(rpair.at[k, 1 - core], rcore.at[k], x_send.at[k], x_recv.at[k], (other, me_t))
        c.start()
        xcopies.append(c)
    zcopies = []
    for k in range(nz):
        z = peer_z(k + 1)
        xcopies[k].wait()
        rpart[k] = rpair[k, core] + rcore[k]
        if k < nz - 1:
            c = send(rpart.at[k], rgot.at[k], z_send.at[k], z_recv.at[k], (z * 2 + core, me_t))
            c.start()
            zcopies.append(c)
    total = dot(mix[me_t], tr[...].reshape(cols, d), NN) * SCALE
    for k in range(1, nt):
        lcopies[k - 1].wait()
        total = total + lgot[k]
    out_s[...] = total
    total = rpart[nz - 1]
    for k in range(nz - 1):
        zcopies[k].wait()
        total = total + rgot[k]
    out_t[...] = total


def per_device(ns, nt, src_emb, right_sentence_vectors, src_mass, tgt_mass):
    bs, d = src_emb.shape
    bt = right_sentence_vectors.shape[0]
    rows, cols = nt * bs, ns * bt
    nz = ns // 2
    dma = pltpu.SemaphoreType.DMA
    v = pltpu.VMEM
    scratch = [
        v((nt, bs, d), BF16), v((ns, bt, d), BF16),
        v((nt, bs, cols), F32), v((nt, bs, cols), BF16), v((nt, bs, cols), BF16),
        v((nt, bs, cols), BF16), v((nt, bs, cols), BF16),
        v((nt, bs, d), F32), v((nz, 2, bt, d), F32), v((nz, bt, d), F32), v((nt, bs, d), F32),
        v((nz, bt, d), F32), v((nz, bt, d), F32),
        v((2 * ITERS, rows), F32), v((2 * ITERS, cols), F32), v((8, rows), F32), v((8, cols), F32),
        v((2 * ITERS, nt, 1, rows), F32), v((2 * ITERS - 2, ns, 1, cols), F32),
        v((ns, 1, 2 * cols), F32),
        dma((nt,)), dma((nt,)), dma((nz,)), dma((nz,)), dma((nz,)), dma((nz,)),
        dma((2 * ITERS, nt)), dma((2 * ITERS, nt)),
        dma((2 * ITERS - 2, ns)), dma((2 * ITERS - 2, ns)), dma((ns,)), dma((ns,)),
        dma((nt,)), dma((nt,)), dma((nz,)), dma((nz,)), dma((nz,)), dma((nz,)),
    ]
    vm = pl.BlockSpec(memory_space=pltpu.VMEM)
    return pl.pallas_call(
        functools.partial(body, ns, nt),
        out_shape=(jax.ShapeDtypeStruct((bs, d), F32), jax.ShapeDtypeStruct((bt, d), F32)),
        in_specs=[vm] * 4,
        out_specs=(vm, vm),
        scratch_shapes=scratch,
        compiler_params=pltpu.CompilerParams(
            collective_id=0, has_side_effects=True, vmem_limit_bytes=50 * 1024 * 1024
        ),
    )(src_emb, right_sentence_vectors, src_mass.reshape(1, rows), tgt_mass.reshape(1, cols))


def solution(mesh):
    ns, nt = mesh.shape["src"], mesh.shape["tgt"]
    placed = (P(("src", "tgt"), None), P(("tgt", "src"), None), P("src"), P("tgt"))
    return jax.shard_map(
        functools.partial(per_device, ns, nt),
        mesh=mesh,
        in_specs=placed,
        out_specs=(P(("src", "tgt"), None), P(("tgt", "src"), None)),
        check_vma=False,
    )
```

```python
import functools
import jax
import jax.numpy as jnp
from jax import lax
from jax.experimental import pallas as pl
from jax.experimental.pallas import tpu as pltpu
from jax.sharding import PartitionSpec as P

ITERS = 4
SCALE = 20.0
SPAN = 80.0
TINY = 1e-30
F32 = jnp.float32
BF16 = jnp.bfloat16
NN = (((1,), (0,)), ((), ()))
NT = (((1,), (1,)), ((), ()))
TN = (((0,), (0,)), ((), ()))
MESH = pl.DeviceIdType.MESH


def dot(a, b, dims):
    return lax.dot_general(a, b, dims, preferred_element_type=F32)


def split3(x):
    hi = x.astype(BF16).astype(F32)
    rest = x - hi
    mid = rest.astype(BF16).astype(F32)
    low = (rest - mid).astype(BF16).astype(F32)
    return hi, mid, low


def three_rows(x):
    hi, mid, low = split3(x)
    shape = (16, x.shape[1])
    row = lax.broadcasted_iota(jnp.int32, shape, 0)
    full = [jnp.broadcast_to(p, shape) for p in (hi, mid, low)]
    zero = jnp.zeros(shape, F32)
    return jnp.where(
        row == 0, full[0], jnp.where(row == 1, full[1], jnp.where(row == 2, full[2], zero))
    ).astype(BF16)


def encode(x):
    m = jnp.maximum(jnp.max(jnp.abs(x), axis=0, keepdims=True), TINY)
    return jnp.exp(x * (SPAN / m)).astype(BF16), m * (1.0 / SPAN)


def decode(y, m):
    return jnp.log(y.astype(F32)) * m


def body(
    ns, nt, src_ref, tgt_ref, smass_hbm, tmass_hbm, out_s, out_t, smass_ref, tmass_ref, own_sem,
    sr, tr, aff, ker, w1, w2, mix, lpart, rpair, rpart, lgot, rcore, rgot, lscale, lsgot, rscale, rsgot,
    ru, vc, rsum, csum, rbuf, cbuf,
    gs_send, gs_recv, gt_send, gt_recv, gc_send, gc_recv,
    r_send, r_recv, c_send, c_recv,
    l_send, l_recv, x_send, x_recv, z_send, z_recv,
    ls_send, ls_recv, zs_send, zs_recv,
):
    me_t = lax.axis_index("tgt")
    me_s = lax.axis_index("src")
    nz = ns // 2
    core = lax.rem(me_s, 2)
    me_z = lax.div(me_s, 2)
    other = me_z * 2 + (1 - core)
    bs, d = src_ref.shape
    bt = tgt_ref.shape[0]
    rows, cols = nt * bs, ns * bt

    def peer_t(k):
        return lax.rem(me_t + k, nt)

    def peer_s(k):
        return lax.rem(me_s + k, ns)

    def peer_z(k):
        return lax.rem(me_z + k, nz)

    barrier = pltpu.get_barrier_semaphore()
    for k in range(1, nt):
        pl.semaphore_signal(barrier, inc=1, device_id=(me_s, peer_t(k)), device_id_type=MESH)
    for k in range(1, ns):
        pl.semaphore_signal(barrier, inc=1, device_id=(peer_s(k), me_t), device_id_type=MESH)
    pl.semaphore_wait(barrier, nt + ns - 2)

    def send(src, dst, s_sem, r_sem, dev):
        return pltpu.make_async_remote_copy(
            src_ref=src, dst_ref=dst, send_sem=s_sem, recv_sem=r_sem,
            device_id=dev, device_id_type=MESH,
        )

    own = [
        pltpu.make_async_copy(src_ref, sr.at[me_t], own_sem.at[0]),
        pltpu.make_async_copy(tgt_ref, tr.at[me_s], own_sem.at[1]),
        pltpu.make_async_copy(smass_hbm, smass_ref, own_sem.at[2]),
        pltpu.make_async_copy(tmass_hbm, tmass_ref, own_sem.at[3]),
    ]
    gz = [
        send(tgt_ref, tr.at[me_s], gt_send.at[k], gt_recv.at[k], (peer_z(k) * 2 + core, me_t))
        for k in range(1, nz)
    ]
    gt = [
        send(src_ref, sr.at[me_t], gs_send.at[k], gs_recv.at[k], (me_s, peer_t(k)))
        for k in range(1, nt)
    ]
    for c in gz + gt:
        c.start()
    fwd = [send(tgt_ref, tr.at[me_s], gc_send.at[0], gc_recv.at[0], (other, me_t))]
    fwd[0].start()
    for c in own:
        c.start()
    for k in range(1, nz):
        gz[k - 1].wait_recv()
        blk = lax.rem(me_z + nz - k, nz) * 2 + core
        c = send(tr.at[blk], tr.at[blk], gc_send.at[k], gc_recv.at[k], (other, me_t))
        c.start()
        fwd.append(c)
    for c in own + gt + fwd:
        c.wait()
    for c in gz:
        c.wait_send()

    def build(i, carry):
        a = dot(sr[i], tr[...].reshape(cols, d), NT) * SCALE
        ker[i] = jnp.exp(a).astype(BF16)
        aff[i] = a
        return carry

    def weigh(k):
        for j in range(nt // ITERS):
            i = k * (nt // ITERS) + j
            w = ker[i].astype(F32) * aff[i]
            h = w.astype(BF16)
            w1[i] = h
            w2[i] = (w - h.astype(F32)).astype(BF16)

    lax.fori_loop(0, nt, build, 0)

    def row_pass(m, x):
        return jnp.sum(dot(three_rows(x), m[...].reshape(rows, cols), NT), axis=0, keepdims=True)

    def col_pass(m, x):
        return jnp.sum(dot(three_rows(x), m[...].reshape(rows, cols), NN), axis=0, keepdims=True)

    def row_total(step, part, during=None):
        rbuf[step, me_t] = part
        cs = [
            send(rbuf.at[step, me_t], rbuf.at[step, me_t], r_send.at[step, k], r_recv.at[step, k],
                 (me_s, peer_t(k)))
            for k in range(1, nt)
        ]
        for c in cs:
            c.start()
        if during is not None:
            during()
        for c in cs:
            c.wait()
        total = rbuf[step, 0]
        for i in range(1, nt):
            total = total + rbuf[step, i]
        return total

    def col_start(step, part):
        cbuf[step, me_s] = part
        cs = [
            send(cbuf.at[step, me_s], cbuf.at[step, me_s], c_send.at[step, k], c_recv.at[step, k],
                 (peer_s(k), me_t))
            for k in range(1, ns)
        ]
        for c in cs:
            c.start()
        return cs

    def col_done(step, cs):
        for c in cs:
            c.wait()
        total = cbuf[step, 0]
        for i in range(1, ns):
            total = total + cbuf[step, i]
        return total

    def col_total(step, part):
        return col_done(step, col_start(step, part))

    vc[pl.ds(0, 1), :] = jnp.ones((1, cols), F32)

    def scale_src(k):
        r = row_total(k, row_pass(ker, vc[pl.ds(k, 1), :]), lambda: weigh(k))
        u = smass_ref[...] / r
        rsum[pl.ds(k, 1), :] = r
        ru[pl.ds(ITERS + k, 1), :] = u
        return u

    def forward(k, carry):
        u = scale_src(k)
        c = col_total(k, col_pass(ker, u))
        csum[pl.ds(k, 1), :] = c
        vc[pl.ds(k + 1, 1), :] = tmass_ref[...] / c
        return carry

    lax.fori_loop(0, ITERS - 1, forward, 0)
    last = ITERS - 1
    u4 = scale_src(last)
    first = col_start(last, col_pass(ker, u4))
    second = col_start(2 * last + 1, col_pass(w1, u4) + col_pass(w2, u4))
    c4 = col_done(last, first)
    v4 = tmass_ref[...] / c4
    src_adj = row_pass(w1, v4) + row_pass(w2, v4)
    tgt_adj = col_done(2 * last + 1, second)
    cbar = -tgt_adj * v4 / c4
    vc[pl.ds(ITERS + last, 1), :] = cbar
    part = row_pass(ker, cbar) + src_adj

    def rbar_of(k, part):
        back = row_total(ITERS + k, part)
        rbar = -back * ru[pl.ds(ITERS + k, 1), :] / rsum[pl.ds(k, 1), :]
        ru[pl.ds(k, 1), :] = rbar
        return rbar

    rbar = rbar_of(last, part)

    def backward(j, rbar):
        k = last - 1 - j
        adj = col_total(ITERS + j, col_pass(ker, rbar))
        cbar = -adj * vc[pl.ds(k + 1, 1), :] / csum[pl.ds(k, 1), :]
        vc[pl.ds(ITERS + k, 1), :] = cbar
        return rbar_of(k, row_pass(ker, cbar))

    lax.fori_loop(0, ITERS - 1, backward, rbar)

    lh, lm, ll = split3(ru[...])
    rh, rm, rl = split3(vc[...])
    zero = jnp.zeros((8, cols), F32)
    lstack = jnp.concatenate(
        [lh, lh, lm, lm, lh, ll, jnp.broadcast_to(u4, (8, rows)), jnp.zeros((8, rows), F32)], axis=0
    )
    lcol = lstack.T
    rstack = jnp.concatenate([rh, rm, rh, rm, rl, rh, zero, zero], axis=0).astype(BF16)
    for i in range(nt):
        blk = lcol[i * bs:(i + 1) * bs]
        lk = blk.astype(BF16)
        low = dot(lk, rstack, NN)
        ucol = blk[:, 48:49]
        m = ker[i].astype(F32) * (ucol * v4 * (1.0 + aff[i]) + low)
        mix[i] = m.astype(BF16)

    lcopies = []
    xcopies = []
    zcopies = []

    def left(k):
        i = peer_t(k)
        lpart[k], lscale[k] = encode(dot(mix[i], tr[...].reshape(cols, d), NN) * SCALE)
        lcopies.append(send(lpart.at[k], lgot.at[k], l_send.at[k], l_recv.at[k], (me_s, i)))
        lcopies.append(send(lscale.at[k], lsgot.at[k], ls_send.at[k], ls_recv.at[k], (me_s, i)))
        lcopies[-2].start()
        lcopies[-1].start()

    def right(k):
        z = peer_z(k + 1)
        m = mix[:, :, pl.ds(pl.multiple_of(z * (2 * bt), 2 * bt), 2 * bt)].reshape(rows, 2 * bt)
        pair = dot(m, sr[...].reshape(rows, d), TN) * SCALE
        rpair[k] = pair.reshape(2, bt, d)
        c = send(rpair.at[k, 1 - core], rcore.at[k], x_send.at[k], x_recv.at[k], (other, me_t))
        c.start()
        xcopies.append(c)

    def along_z(k):
        z = peer_z(k + 1)
        xcopies[k].wait()
        rpart[k], rscale[k] = encode(rpair[k, core] + rcore[k])
        dev = (z * 2 + core, me_t)
        zcopies.append(send(rpart.at[k], rgot.at[k], z_send.at[k], z_recv.at[k], dev))
        zcopies.append(send(rscale.at[k], rsgot.at[k], zs_send.at[k], zs_recv.at[k], dev))
        zcopies[-2].start()
        zcopies[-1].start()

    right(0)
    left(1)
    for k in range(1, nz):
        right(k)
        along_z(k - 1)
        if k + 1 < nt:
            left(k + 1)
    for k in range(nz + 1, nt):
        left(k)
    total = dot(mix[me_t], tr[...].reshape(cols, d), NN) * SCALE
    for k in range(1, nt):
        lcopies[2 * k - 2].wait()
        lcopies[2 * k - 1].wait()
        total = total + decode(lgot[k], lsgot[k])
    out_s[...] = total
    xcopies[nz - 1].wait()
    total = rpair[nz - 1, core] + rcore[nz - 1]
    for k in range(nz - 1):
        zcopies[2 * k].wait()
        zcopies[2 * k + 1].wait()
        total = total + decode(rgot[k], rsgot[k])
    out_t[...] = total


def per_device(ns, nt, src_emb, right_sentence_vectors, src_mass, tgt_mass):
    bs, d = src_emb.shape
    bt = right_sentence_vectors.shape[0]
    rows, cols = nt * bs, ns * bt
    nz = ns // 2
    dma = pltpu.SemaphoreType.DMA
    v = pltpu.VMEM
    scratch = [
        v((1, rows), F32), v((1, cols), F32), dma((4,)),
        v((nt, bs, d), BF16), v((ns, bt, d), BF16),
        v((nt, bs, cols), F32), v((nt, bs, cols), BF16), v((nt, bs, cols), BF16),
        v((nt, bs, cols), BF16), v((nt, bs, cols), BF16),
        v((nt, bs, d), BF16), v((nz, 2, bt, d), F32), v((nz, bt, d), BF16), v((nt, bs, d), BF16),
        v((nz, bt, d), F32), v((nz, bt, d), BF16),
        v((nt, 1, d), F32), v((nt, 1, d), F32), v((nz, 1, d), F32), v((nz, 1, d), F32),
        v((2 * ITERS, rows), F32), v((2 * ITERS, cols), F32), v((8, rows), F32), v((8, cols), F32),
        v((2 * ITERS, nt, 1, rows), F32), v((2 * ITERS, ns, 1, cols), F32),
        dma((nt,)), dma((nt,)), dma((nz,)), dma((nz,)), dma((nz,)), dma((nz,)),
        dma((2 * ITERS, nt)), dma((2 * ITERS, nt)),
        dma((2 * ITERS, ns)), dma((2 * ITERS, ns)),
        dma((nt,)), dma((nt,)), dma((nz,)), dma((nz,)), dma((nz,)), dma((nz,)),
        dma((nt,)), dma((nt,)), dma((nz,)), dma((nz,)),
    ]
    vm = pl.BlockSpec(memory_space=pltpu.VMEM)
    return pl.pallas_call(
        functools.partial(body, ns, nt),
        out_shape=(jax.ShapeDtypeStruct((bs, d), F32), jax.ShapeDtypeStruct((bt, d), F32)),
        in_specs=[pl.BlockSpec(memory_space=pl.ANY)] * 4,
        out_specs=(vm, vm),
        scratch_shapes=scratch,
        compiler_params=pltpu.CompilerParams(
            collective_id=0, has_side_effects=True, vmem_limit_bytes=50 * 1024 * 1024
        ),
    )(src_emb, right_sentence_vectors, src_mass.reshape(1, rows), tgt_mass.reshape(1, cols))


def solution(mesh):
    ns, nt = mesh.shape["src"], mesh.shape["tgt"]
    placed = (P(("src", "tgt"), None), P(("tgt", "src"), None), P("src"), P("tgt"))
    return jax.shard_map(
        functools.partial(per_device, ns, nt),
        mesh=mesh,
        in_specs=placed,
        out_specs=(P(("src", "tgt"), None), P(("tgt", "src"), None)),
        check_vma=False,
    )
```

```python
import functools
import jax
import jax.numpy as jnp
from jax import lax
from jax.experimental import pallas as pl
from jax.experimental.pallas import tpu as pltpu
from jax.sharding import PartitionSpec as P

ITERS = 4
SCALE = 20.0
SPAN = 80.0
TINY = 1e-30
F32 = jnp.float32
BF16 = jnp.bfloat16
NN = (((1,), (0,)), ((), ()))
NT = (((1,), (1,)), ((), ()))
TN = (((0,), (0,)), ((), ()))
MESH = pl.DeviceIdType.MESH


def dot(a, b, dims):
    return lax.dot_general(a, b, dims, preferred_element_type=F32)


def split3(x):
    hi = x.astype(BF16).astype(F32)
    rest = x - hi
    mid = rest.astype(BF16).astype(F32)
    low = (rest - mid).astype(BF16).astype(F32)
    return hi, mid, low


def three_rows(x):
    hi, mid, low = split3(x)
    shape = (16, x.shape[1])
    row = lax.broadcasted_iota(jnp.int32, shape, 0)
    full = [jnp.broadcast_to(p, shape) for p in (hi, mid, low)]
    zero = jnp.zeros(shape, F32)
    return jnp.where(
        row == 0, full[0], jnp.where(row == 1, full[1], jnp.where(row == 2, full[2], zero))
    ).astype(BF16)


def encode(x):
    m = jnp.maximum(jnp.max(jnp.abs(x), axis=0, keepdims=True), TINY)
    return jnp.exp(x * (SPAN / m)).astype(BF16), m * (1.0 / SPAN)


def decode(y, m):
    return jnp.log(y.astype(F32)) * m


def body(
    ns, nt, src_ref, tgt_ref, smass_hbm, tmass_hbm, out_s, out_t, smass_ref, tmass_ref, own_sem,
    sr, tr, aff, ker, w1, w2, mix, lpart, rpair, rpart, lgot, rcore, rgot, lscale, lsgot, rscale, rsgot,
    ru, vc, rsum, csum, rbuf, cbuf,
    gs_send, gs_recv, gt_send, gt_recv, gc_send, gc_recv,
    r_send, r_recv, c_send, c_recv,
    l_send, l_recv, x_send, x_recv, z_send, z_recv,
    ls_send, ls_recv, zs_send, zs_recv,
):
    me_t = lax.axis_index("tgt")
    me_s = lax.axis_index("src")
    nz = ns // 2
    core = lax.rem(me_s, 2)
    me_z = lax.div(me_s, 2)
    other = me_z * 2 + (1 - core)
    bs, d = src_ref.shape
    bt = tgt_ref.shape[0]
    rows, cols = nt * bs, ns * bt

    def peer_t(k):
        return lax.rem(me_t + k, nt)

    def peer_s(k):
        return lax.rem(me_s + k, ns)

    def peer_z(k):
        return lax.rem(me_z + k, nz)

    barrier = pltpu.get_barrier_semaphore()
    for k in range(1, nt):
        pl.semaphore_signal(barrier, inc=1, device_id=(me_s, peer_t(k)), device_id_type=MESH)
    for k in range(1, ns):
        pl.semaphore_signal(barrier, inc=1, device_id=(peer_s(k), me_t), device_id_type=MESH)
    pl.semaphore_wait(barrier, nt + ns - 2)

    def send(src, dst, s_sem, r_sem, dev):
        return pltpu.make_async_remote_copy(
            src_ref=src, dst_ref=dst, send_sem=s_sem, recv_sem=r_sem,
            device_id=dev, device_id_type=MESH,
        )

    own = [
        pltpu.make_async_copy(src_ref, sr.at[me_t], own_sem.at[0]),
        pltpu.make_async_copy(tgt_ref, tr.at[me_s], own_sem.at[1]),
        pltpu.make_async_copy(smass_hbm, smass_ref, own_sem.at[2]),
        pltpu.make_async_copy(tmass_hbm, tmass_ref, own_sem.at[3]),
    ]
    gz = [
        send(tgt_ref, tr.at[me_s], gt_send.at[k], gt_recv.at[k], (peer_z(k) * 2 + core, me_t))
        for k in range(1, nz)
    ]
    gt = [
        send(src_ref, sr.at[me_t], gs_send.at[k], gs_recv.at[k], (me_s, peer_t(k)))
        for k in range(1, nt)
    ]
    for c in gz + gt[::-1]:
        c.start()
    fwd = [send(tgt_ref, tr.at[me_s], gc_send.at[0], gc_recv.at[0], (other, me_t))]
    fwd[0].start()
    for c in own:
        c.start()
    for k in range(1, nz):
        gz[k - 1].wait_recv()
        blk = lax.rem(me_z + nz - k, nz) * 2 + core
        c = send(tr.at[blk], tr.at[blk], gc_send.at[k], gc_recv.at[k], (other, me_t))
        c.start()
        fwd.append(c)
    for c in own + gt:
        c.wait()
    for c in gz:
        c.wait_send()

    def build(z):
        at = pl.ds(pl.multiple_of(z * (2 * bt), 2 * bt), 2 * bt)
        pair = tr[pl.ds(2 * z, 2)].reshape(2 * bt, d)

        def rows_of(i, carry):
            a = dot(sr[i], pair, NT) * SCALE
            ker[i, :, at] = jnp.exp(a).astype(BF16)
            aff[i, :, at] = a
            return carry

        lax.fori_loop(0, nt, rows_of, 0, unroll=True)

    for k in range(nz):
        fwd[k].wait()
        build(lax.rem(me_z + nz - k, nz))

    def weigh(k):
        for j in range(nt // ITERS):
            i = k * (nt // ITERS) + j
            w = ker[i].astype(F32) * aff[i]
            h = w.astype(BF16)
            w1[i] = h
            w2[i] = (w - h.astype(F32)).astype(BF16)


    def row_pass(m, x):
        return jnp.sum(dot(three_rows(x), m[...].reshape(rows, cols), NT), axis=0, keepdims=True)

    def col_pass(m, x):
        return jnp.sum(dot(three_rows(x), m[...].reshape(rows, cols), NN), axis=0, keepdims=True)

    def row_total(step, part, during=None):
        rbuf[step, me_t] = part
        cs = [
            send(rbuf.at[step, me_t], rbuf.at[step, me_t], r_send.at[step, k], r_recv.at[step, k],
                 (me_s, peer_t(k)))
            for k in range(1, nt)
        ]
        for c in cs:
            c.start()
        if during is not None:
            during()
        for c in cs:
            c.wait()
        total = rbuf[step, 0]
        for i in range(1, nt):
            total = total + rbuf[step, i]
        return total

    def col_start(step, part):
        cbuf[step, me_s] = part
        cs = [
            send(cbuf.at[step, me_s], cbuf.at[step, me_s], c_send.at[step, k], c_recv.at[step, k],
                 (peer_s(k), me_t))
            for k in range(1, ns)
        ]
        for c in cs:
            c.start()
        return cs

    def col_done(step, cs):
        for c in cs:
            c.wait()
        total = cbuf[step, 0]
        for i in range(1, ns):
            total = total + cbuf[step, i]
        return total

    def col_total(step, part):
        return col_done(step, col_start(step, part))

    vc[pl.ds(0, 1), :] = jnp.ones((1, cols), F32)

    def scale_src(k):
        r = row_total(k, row_pass(ker, vc[pl.ds(k, 1), :]), lambda: weigh(k))
        u = smass_ref[...] / r
        rsum[pl.ds(k, 1), :] = r
        ru[pl.ds(ITERS + k, 1), :] = u
        return u

    def forward(k, carry):
        u = scale_src(k)
        c = col_total(k, col_pass(ker, u))
        csum[pl.ds(k, 1), :] = c
        vc[pl.ds(k + 1, 1), :] = tmass_ref[...] / c
        return carry

    lax.fori_loop(0, ITERS - 1, forward, 0)
    last = ITERS - 1
    u4 = scale_src(last)
    first = col_start(last, col_pass(ker, u4))
    second = col_start(2 * last + 1, col_pass(w1, u4) + col_pass(w2, u4))
    c4 = col_done(last, first)
    v4 = tmass_ref[...] / c4
    src_adj = row_pass(w1, v4) + row_pass(w2, v4)
    tgt_adj = col_done(2 * last + 1, second)
    cbar = -tgt_adj * v4 / c4
    vc[pl.ds(ITERS + last, 1), :] = cbar
    part = row_pass(ker, cbar) + src_adj

    def rbar_of(k, part, during=None):
        back = row_total(ITERS + k, part, during)
        rbar = -back * ru[pl.ds(ITERS + k, 1), :] / rsum[pl.ds(k, 1), :]
        ru[pl.ds(k, 1), :] = rbar
        return rbar

    rbar = rbar_of(last, part)

    def backward(j, rbar):
        k = last - 1 - j
        adj = col_total(ITERS + j, col_pass(ker, rbar))
        cbar = -adj * vc[pl.ds(k + 1, 1), :] / csum[pl.ds(k, 1), :]
        vc[pl.ds(ITERS + k, 1), :] = cbar
        return rbar_of(k, row_pass(ker, cbar))

    rbar = lax.fori_loop(0, ITERS - 2, backward, rbar)
    ru[pl.ds(0, 1), :] = jnp.zeros((1, rows), F32)
    adj = col_total(ITERS + last - 1, col_pass(ker, rbar))
    cbar = -adj * vc[pl.ds(1, 1), :] / csum[pl.ds(0, 1), :]
    vc[pl.ds(ITERS, 1), :] = cbar

    def base():
        lh, lm, ll = split3(ru[...])
        rh, rm, rl = split3(vc[...])
        zero = jnp.zeros((8, cols), F32)
        lstack = jnp.concatenate(
            [lh, lh, lm, lm, lh, ll, jnp.broadcast_to(u4, (8, rows)), jnp.zeros((8, rows), F32)],
            axis=0,
        )
        lcol = lstack.T
        rstack = jnp.concatenate([rh, rm, rh, rm, rl, rh, zero, zero], axis=0).astype(BF16)
        for i in range(nt):
            blk = lcol[i * bs:(i + 1) * bs]
            low = dot(blk.astype(BF16), rstack, NN)
            aff[i] = blk[:, 48:49] * v4 * (1.0 + aff[i]) + low

    rbar = rbar_of(0, row_pass(ker, cbar), base)
    rcol = jnp.broadcast_to(rbar, (8, rows)).T
    for i in range(nt):
        m = ker[i].astype(F32) * (aff[i] + rcol[i * bs:(i + 1) * bs, 0:1])
        mix[i] = m.astype(BF16)

    lcopies = {}
    xcopies = []
    zcopies = []

    def left(k):
        i = peer_t(k)
        lpart[k], lscale[k] = encode(dot(mix[i], tr[...].reshape(cols, d), NN) * SCALE)
        lcopies[k] = (
            send(lpart.at[k], lgot.at[k], l_send.at[k], l_recv.at[k], (me_s, i)),
            send(lscale.at[k], lsgot.at[k], ls_send.at[k], ls_recv.at[k], (me_s, i)),
        )
        for c in lcopies[k]:
            c.start()

    def right(k):
        z = peer_z(k + 1)
        m = mix[:, :, pl.ds(pl.multiple_of(z * (2 * bt), 2 * bt), 2 * bt)].reshape(rows, 2 * bt)
        pair = dot(m, sr[...].reshape(rows, d), TN) * SCALE
        rpair[k] = pair.reshape(2, bt, d)
        c = send(rpair.at[k, 1 - core], rcore.at[k], x_send.at[k], x_recv.at[k], (other, me_t))
        c.start()
        xcopies.append(c)

    def along_z(k):
        z = peer_z(k + 1)
        xcopies[k].wait()
        rpart[k], rscale[k] = encode(rpair[k, core] + rcore[k])
        dev = (z * 2 + core, me_t)
        zcopies.append(send(rpart.at[k], rgot.at[k], z_send.at[k], z_recv.at[k], dev))
        zcopies.append(send(rscale.at[k], rsgot.at[k], zs_send.at[k], zs_recv.at[k], dev))
        zcopies[-2].start()
        zcopies[-1].start()

    left(nt - 1)
    right(0)
    if nt > 2:
        left(nt - 2)
    for k in range(1, nz):
        right(k)
        along_z(k - 1)
        if k + 2 < nt:
            left(nt - 2 - k)
    for k in range(nz + 2, nt):
        left(nt - k)
    total = dot(mix[me_t], tr[...].reshape(cols, d), NN) * SCALE
    for k in range(1, nt):
        for c in lcopies[k]:
            c.wait()
        total = total + decode(lgot[k], lsgot[k])
    out_s[...] = total
    xcopies[nz - 1].wait()
    total = rpair[nz - 1, core] + rcore[nz - 1]
    for k in range(nz - 1):
        zcopies[2 * k].wait()
        zcopies[2 * k + 1].wait()
        total = total + decode(rgot[k], rsgot[k])
    out_t[...] = total


def per_device(ns, nt, src_emb, right_sentence_vectors, src_mass, tgt_mass):
    bs, d = src_emb.shape
    bt = right_sentence_vectors.shape[0]
    rows, cols = nt * bs, ns * bt
    nz = ns // 2
    dma = pltpu.SemaphoreType.DMA
    v = pltpu.VMEM
    scratch = [
        v((1, rows), F32), v((1, cols), F32), dma((4,)),
        v((nt, bs, d), BF16), v((ns, bt, d), BF16),
        v((nt, bs, cols), F32), v((nt, bs, cols), BF16), v((nt, bs, cols), BF16),
        v((nt, bs, cols), BF16), v((nt, bs, cols), BF16),
        v((nt, bs, d), BF16), v((nz, 2, bt, d), F32), v((nz, bt, d), BF16), v((nt, bs, d), BF16),
        v((nz, bt, d), F32), v((nz, bt, d), BF16),
        v((nt, 1, d), F32), v((nt, 1, d), F32), v((nz, 1, d), F32), v((nz, 1, d), F32),
        v((2 * ITERS, rows), F32), v((2 * ITERS, cols), F32), v((8, rows), F32), v((8, cols), F32),
        v((2 * ITERS, nt, 1, rows), F32), v((2 * ITERS, ns, 1, cols), F32),
        dma((nt,)), dma((nt,)), dma((nz,)), dma((nz,)), dma((nz,)), dma((nz,)),
        dma((2 * ITERS, nt)), dma((2 * ITERS, nt)),
        dma((2 * ITERS, ns)), dma((2 * ITERS, ns)),
        dma((nt,)), dma((nt,)), dma((nz,)), dma((nz,)), dma((nz,)), dma((nz,)),
        dma((nt,)), dma((nt,)), dma((nz,)), dma((nz,)),
    ]
    vm = pl.BlockSpec(memory_space=pltpu.VMEM)
    return pl.pallas_call(
        functools.partial(body, ns, nt),
        out_shape=(jax.ShapeDtypeStruct((bs, d), F32), jax.ShapeDtypeStruct((bt, d), F32)),
        in_specs=[pl.BlockSpec(memory_space=pl.ANY)] * 4,
        out_specs=(vm, vm),
        scratch_shapes=scratch,
        compiler_params=pltpu.CompilerParams(
            collective_id=0, has_side_effects=True, vmem_limit_bytes=50 * 1024 * 1024
        ),
    )(src_emb, right_sentence_vectors, src_mass.reshape(1, rows), tgt_mass.reshape(1, cols))


def solution(mesh):
    ns, nt = mesh.shape["src"], mesh.shape["tgt"]
    placed = (P(("src", "tgt"), None), P(("tgt", "src"), None), P("src"), P("tgt"))
    return jax.shard_map(
        functools.partial(per_device, ns, nt),
        mesh=mesh,
        in_specs=placed,
        out_specs=(P(("src", "tgt"), None), P(("tgt", "src"), None)),
        check_vma=False,
    )
```
